32 devices in a mesh: ctx: 16 (over z, y, core), fsdp: 2 (over x).
Axes of the slice: x: 2, y: 2, z: 4, core: 2. Of those that a mesh axis runs over, the one named last changes fastest.
Arguments:
- layer_input: bfloat16 [8, 2048, 960], P('fsdp', 'ctx'), may hold values from -6 to 6
- out_grad: bfloat16 [8, 2048, 960], P('fsdp', 'ctx'), may hold values from -6 to 6
- attn_gain: bfloat16 [960], P('fsdp'), may hold values from 0.5 to 1.5
- w_query: bfloat16 [960, 960], P('fsdp'), may hold values from -0.1875 to 0.1875
- w_key: bfloat16 [960, 320], P('fsdp'), may hold values from -0.1875 to 0.1875
- w_value: bfloat16 [960, 320], P('fsdp'), may hold values from -0.1875 to 0.1875
- w_output: bfloat16 [960, 960], P('fsdp'), may hold values from -6 to 6
- mlp_gain: bfloat16 [960], P('fsdp'), may hold values from 0.5 to 1.5
- w_gate: bfloat16 [960, 2560], P('fsdp'), may hold values from -0.1875 to 0.1875
- w_up: bfloat16 [960, 2560], P('fsdp'), may hold values from -0.1875 to 0.1875
- w_down: bfloat16 [2560, 960], P('fsdp'), may hold values from -0.125 to 0.125
Outputs:
- layer_output: bfloat16 [8, 2048, 960], P('fsdp', 'ctx')
- input_grad: bfloat16 [8, 2048, 960], P('fsdp', 'ctx')
- attn_gain_grad: float32 [960], P('fsdp')
- w_query_grad: float32 [960, 960], P('fsdp')
- w_key_grad: float32 [960, 320], P('fsdp')
- w_value_grad: float32 [960, 320], P('fsdp')
- w_output_grad: float32 [960, 960], P('fsdp')
- mlp_gain_grad: float32 [960], P('fsdp')
- w_gate_grad: float32 [960, 2560], P('fsdp')
- w_up_grad: float32 [960, 2560], P('fsdp')
- w_down_grad: float32 [2560, 960], P('fsdp')
The draws below stay inside these ranges and needn't reach their ends.
All inputs are finite; a program needn't handle non-finite values.
Results may differ from the reference program's by a relative error of at most 0.034.
Values may be sent and summed in bfloat16 or wider, within the bound.
A program may use at most 256 MiB of HBM per device.

```python
import jax
import jax.numpy as jnp
from jax import lax

D = 960
QH = 15
KVH = 5
HD = 64
FF = 2560
BLK = 64
BLOCKS = 32
L = 2048
SEQS = 8
N_CTX = 16


def levels(own_key, extent, pieces, low, largest):
    loudness, own = 1.0, jax.random.fold_in(own_key, 6)
    for axis_at, parts in pieces:
        draws = jnp.exp(jax.random.uniform(jax.random.fold_in(own, axis_at), (parts,), jnp.float32, low / len(pieces), largest / len(pieces)))
        loudness = loudness * jnp.repeat(draws, extent[axis_at] // parts).reshape([-1 if axis == axis_at else 1 for axis in range(len(extent))])
    return loudness


def normal_values(own_key, extent, width, bound, cuts=(), held_as=jnp.bfloat16):
    entries = width * jax.random.normal(own_key, extent, jnp.float32)
    if cuts:
        entries = entries * levels(own_key, extent, cuts, -0.22, 0.18)
    return jnp.clip(entries, -bound, bound).astype(held_as)


def setup_inputs(seed: int = 0) -> dict:
    key_of = jax.random.split(jax.random.key(seed), 12)
    layer_input = normal_values(key_of[0], (SEQS, L, D), 1.0, 6.0, ((0, 2), (1, 16)))
    out_grad = normal_values(key_of[1], (SEQS, L, D), 1.0, 6.0, ((0, 2), (1, 16)))
    attn_gain = jnp.clip(1.0 + 0.1 * jax.random.normal(key_of[2], (D,), jnp.float32), 0.5, 1.5).astype(jnp.bfloat16)
    w_query = normal_values(key_of[3], (D, QH * HD), D ** -0.5, 0.1875, ((0, 2),))
    w_key = normal_values(key_of[4], (D, KVH * HD), D ** -0.5, 0.1875, ((0, 2),))
    w_value = normal_values(key_of[5], (D, KVH * HD), D ** -0.5, 0.1875, ((0, 2),))
    w_output = normal_values(key_of[6], (QH * HD, D), ((BLK * N_CTX // 2) ** 0.5 * (QH * HD) ** -0.5), 6.0, ((0, 2),))
    mlp_gain = jnp.clip(1.0 + 0.1 * jax.random.normal(key_of[7], (D,), jnp.float32), 0.5, 1.5).astype(jnp.bfloat16)
    w_gate = normal_values(key_of[8], (D, FF), D ** -0.5, 0.1875, ((0, 2),))
    w_up = normal_values(key_of[9], (D, FF), D ** -0.5, 0.1875, ((0, 2),))
    w_down = normal_values(key_of[10], (FF, D), FF ** -0.5, 0.125, ((0, 2),))
    return dict(layer_input=layer_input, out_grad=out_grad, attn_gain=attn_gain, w_query=w_query, w_key=w_key, w_value=w_value, w_output=w_output, mlp_gain=mlp_gain, w_gate=w_gate, w_up=w_up, w_down=w_down)


EPS = 1e-05
THETA = 100000.0
FAR = -1e+30
HIGH = lax.Precision.HIGHEST

@jax.custom_vjp
def low(v):
    return lax.optimization_barrier(v.astype(jnp.bfloat16)).astype(jnp.float32)

@jax.custom_vjp
def low_back(v):
    return v

def low_keep(v):
    return (low(v), None)

def low_pass(kept, grad):
    return (grad,)

def back_keep(v):
    return (v, None)

def back_low(kept, grad):
    return (low(grad),)
low.defvjp(low_keep, low_pass)
low_back.defvjp(back_keep, back_low)

def matmul(left, right):
    return jnp.dot(left, right, precision=HIGH)

def positions_of(total_rows):
    stored = jnp.arange(total_rows, dtype=jnp.int32)
    holder = stored // (2 * BLK)
    within = stored % (2 * BLK)
    mirror = (BLOCKS - 1 - holder) * BLK + within - BLK
    return jnp.where(within < BLK, holder * BLK + within, mirror)

def rotate(values_in, position, heads, sign):
    full_shape = values_in.shape
    by_head = values_in.reshape(full_shape[:-1] + (heads, HD))
    frequency = THETA ** (-jnp.arange(0, HD, 2, dtype=jnp.float32) / HD)
    angles = position.astype(jnp.float32)[:, None] * frequency[None, :]
    cosine = jnp.concatenate([jnp.cos(angles), jnp.cos(angles)], -1)[:, None, :]
    sine_part = sign * jnp.concatenate([jnp.sin(angles), jnp.sin(angles)], -1)[:, None, :]
    first_half = by_head[..., :HD // 2]
    second_half = by_head[..., HD // 2:]
    turned = jnp.concatenate([-second_half, first_half], -1)
    return (by_head * cosine + turned * sine_part).reshape(full_shape)

def normalize(values_in, gain):
    scale_inv = lax.rsqrt(lax.optimization_barrier(jnp.mean(values_in * values_in, -1, keepdims=True)) + EPS)
    return values_in * scale_inv * gain

def attention(queries, keys, values_in, position):
    total_rows = queries.shape[0]
    group_size = QH // KVH
    query_rows = 2 * BLK
    q_blocks = queries.reshape(total_rows // query_rows, query_rows, KVH, group_size, HD)
    p_blocks = position.reshape(total_rows // query_rows, query_rows)
    k_heads = keys.reshape(total_rows, KVH, HD)
    v_heads = values_in.reshape(total_rows, KVH, HD)

    def one_block(operands):
        q_block, p_block = operands
        raw_scores = jnp.einsum('qkgd,tkd->kgqt', q_block, k_heads, precision=HIGH) * HD ** (-0.5)
        raw_scores = low_back(raw_scores)
        allowed = position[None, :] <= p_block[:, None]
        masked = jnp.where(allowed, raw_scores, FAR)
        row_max = lax.optimization_barrier(jnp.max(masked, -1, keepdims=True))
        exp_terms = jnp.where(allowed, jnp.exp(masked - row_max), 0.0)
        prob_full = exp_terms / lax.optimization_barrier(jnp.sum(exp_terms, -1, keepdims=True))
        mixed = jnp.einsum('kgqt,tkd->qkgd', low(prob_full), v_heads, precision=HIGH)
        return mixed.reshape(query_rows, QH * HD)
    outputs = lax.map(jax.checkpoint(one_block), (q_blocks, p_blocks))
    return low(low_back(outputs.reshape(total_rows, QH * HD)))

def layer(weights, sequence, position):
    attn_gain, w_query, w_key, w_value, w_output, mlp_gain, w_gate, w_up, w_down = weights
    normed = low(normalize(sequence, attn_gain))
    queries = low(rotate(low_back(matmul(normed, w_query)), position, QH, 1.0))
    keys = low(rotate(low_back(matmul(normed, w_key)), position, KVH, 1.0))
    values_in = low(low_back(matmul(normed, w_value)))
    attended = attention(queries, keys, values_in, position)
    middle = sequence + low_back(matmul(attended, w_output))
    normed_mid = low(normalize(middle, mlp_gain))
    gate = low_back(matmul(normed_mid, w_gate))
    up_proj = low_back(matmul(normed_mid, w_up))
    hidden = low(jax.nn.silu(gate) * up_proj)
    return middle + low_back(matmul(hidden, w_down))

def forward(layer_in, weights):
    position = positions_of(layer_in.shape[1])
    checked = jax.checkpoint(layer)

    def one_sequence(sequence):
        return checked(weights, sequence, position)
    return lax.map(one_sequence, layer_in)

def reference(layer_input, out_grad, attn_gain, w_query, w_key, w_value, w_output, mlp_gain, w_gate, w_up, w_down):
    weights = tuple((item.astype(jnp.float32) for item in (attn_gain, w_query, w_key, w_value, w_output, mlp_gain, w_gate, w_up, w_down)))
    output, pullback = jax.vjp(forward, layer_input.astype(jnp.float32), weights)
    input_grad, weight_grads = pullback(out_grad.astype(jnp.float32))
    return (output.astype(jnp.bfloat16), input_grad.astype(jnp.bfloat16), weight_grads[0], weight_grads[1], weight_grads[2], weight_grads[3], weight_grads[4], weight_grads[5], weight_grads[6], weight_grads[7], weight_grads[8])
```

```python
import jax
import jax.numpy as jnp
from jax import lax
from jax.experimental import pallas as pl
from jax.experimental.pallas import tpu as pltpu
from jax.sharding import PartitionSpec as P

QH = 15
KVH = 5
HD = 64
GROUP = QH // KVH


EPS = 1e-05
THETA = 100000.0
FAR = -1e30


def place_rows(start_row, row_count, shard_rows, ctx_size):
    stored = start_row + jnp.arange(row_count, dtype=jnp.int32)
    half_rows = shard_rows // 2
    holder = stored // shard_rows
    within = stored % shard_rows
    mirror = (2 * ctx_size - 1 - holder) * half_rows + within - half_rows
    return jnp.where(within < half_rows, holder * half_rows + within, mirror)


def rotate(values_in, position, heads, sign):
    full_shape = values_in.shape
    by_head = values_in.reshape(full_shape[:-1] + (heads, HD))
    frequency = THETA ** (-jnp.arange(0, HD, 2, dtype=jnp.float32) / HD)
    angles = position.astype(jnp.float32)[:, None] * frequency[None, :]
    cosine = jnp.concatenate([jnp.cos(angles), jnp.cos(angles)], -1)[:, None, :]
    sine_part = sign * jnp.concatenate([jnp.sin(angles), jnp.sin(angles)], -1)[:, None, :]
    first_half = by_head[..., : HD // 2]
    second_half = by_head[..., HD // 2 :]
    turned = jnp.concatenate([-second_half, first_half], -1)
    return (by_head * cosine + turned * sine_part).reshape(full_shape)


def outer_sum(left, right):
    return lax.dot_general(
        left, right, (((0, 1), (0, 1)), ((), ())), preferred_element_type=jnp.float32
    )


def times_transposed(grad_in, weight):
    return lax.dot_general(
        grad_in, weight, (((2,), (1,)), ((), ())), preferred_element_type=jnp.float32
    )


def fsdp_gather(shard, half_of_core):
    if lax.axis_size("fsdp") != 2 or lax.axis_size("ctx") % 2:
        return lax.all_gather(shard, "fsdp", axis=0, tiled=True)
    f = lax.axis_index("fsdp")
    rows = shard.shape[0]
    half = rows // 2
    piece = lax.dynamic_slice_in_dim(shard, half_of_core * half, half, 0)
    got = lax.ppermute(piece, "fsdp", [(0, 1), (1, 0)])
    other = xor_permute(got, 1)
    full = jnp.zeros((2 * rows,) + shard.shape[1:], shard.dtype)
    full = lax.dynamic_update_slice_in_dim(full, shard, f * rows, 0)
    start = (1 - f) * rows
    full = lax.dynamic_update_slice_in_dim(full, got, start + half_of_core * half, 0)
    return lax.dynamic_update_slice_in_dim(full, other, start + (1 - half_of_core) * half, 0)


def xor_permute(array, mask):
    size = lax.axis_size("ctx")
    return lax.ppermute(array, "ctx", [(i, i ^ mask) for i in range(size)])


def add_low(kept, received):
    total = kept.astype(jnp.float32) + received.astype(jnp.float32)
    return total.astype(jnp.bfloat16)


def reduce_grad(grad, split_dim):
    grad = grad.astype(jnp.bfloat16)
    size = lax.axis_size("ctx")
    if lax.axis_size("fsdp") != 2 or size & (size - 1) or size < 4:
        part = lax.psum_scatter(grad, "fsdp", scatter_dimension=0, tiled=True)
        return lax.psum(part, "ctx").astype(jnp.float32)
    f = lax.axis_index("fsdp")
    c = lax.axis_index("ctx")
    core = c & 1
    rows, cols = grad.shape
    parts = grad.reshape(2, 2, rows // 4, cols)
    keep = lax.dynamic_index_in_dim(parts, core, 1, False)
    send = lax.dynamic_index_in_dim(parts, 1 - core, 1, False)
    total = add_low(keep, xor_permute(send, 1))
    keep = lax.dynamic_index_in_dim(total, f, 0, False)
    send = lax.dynamic_index_in_dim(total, 1 - f, 0, False)
    total = add_low(keep, lax.ppermute(send, "fsdp", [(0, 1), (1, 0)]))
    masks = []
    mask = 2
    while mask < size:
        masks.append(mask)
        mask *= 2
    for mask in masks[:-1]:
        bit = (c // mask) % 2
        half = total.shape[split_dim] // 2
        keep = lax.dynamic_slice_in_dim(total, bit * half, half, split_dim)
        send = lax.dynamic_slice_in_dim(total, (1 - bit) * half, half, split_dim)
        total = add_low(keep, xor_permute(send, mask))
    total = add_low(total, xor_permute(total, masks[-1]))
    for mask in masks[:-1][::-1]:
        total = join(total, xor_permute(total, mask), (c // mask) % 2, split_dim)
    return join(total, xor_permute(total, 1), core, 0).astype(jnp.float32)


def join(mine, theirs, bit, dim):
    first = jnp.where(bit == 0, mine, theirs)
    second = jnp.where(bit == 0, theirs, mine)
    return jnp.concatenate([first, second], dim)


def gather_order(size, which):
    masks = []
    mask = size // 2
    while mask:
        masks.append(mask)
        mask //= 2
    if which % 2 and len(masks) >= 4:
        masks[1:3] = masks[1:3][::-1]
    return masks


def holders(size, masks):
    offsets = [0]
    for mask in masks:
        offsets = offsets + [offset ^ mask for offset in offsets]
    return jnp.array(offsets, jnp.int32)


def block_parts(kv, pick):
    slots = kv.shape[0] // (4 * HD) * 2
    split = kv.reshape(slots, 2, HD, 2 * HD)
    low = split[:, 0].reshape(slots * HD, 2 * HD)
    high = split[:, 1].reshape(slots * HD, 2 * HD)
    nothing = jnp.zeros((slots * HD, HD), kv.dtype)
    nothing_own = jnp.zeros((2 * HD, HD), kv.dtype)
    rest = 1 - pick

    def of(at):
        lows, highs = low[:, at : at + HD], high[:, at : at + HD]
        return jnp.concatenate(
            [
                jnp.concatenate([lows, nothing], 1),
                jnp.concatenate([highs * pick, lows * rest], 1),
                jnp.concatenate([nothing_own, kv[: 2 * HD, at : at + HD]], 1),
            ],
            0,
        )

    return of(0), of(HD)


def masked_scores(queries, keys, bias, wide):
    scores = lax.dot_general(
        queries, keys, (((1,), (1,)), ((), ())), preferred_element_type=jnp.float32
    )
    step = 2 * HD
    return jnp.concatenate(
        [
            scores[:, :wide],
            scores[:, wide : wide + step] + bias[:, :step],
            scores[:, wide + step : 2 * wide],
            scores[:, 2 * wide :] + bias[:, step:],
        ],
        1,
    )


def spread(high, low):
    shape = (high.shape[0], HD)
    return jnp.concatenate([jnp.broadcast_to(high, shape), jnp.broadcast_to(low, shape)], 1)


def forward_kernel(high_ref, pick_ref, bias_ref, q_ref, kv_ref, out_ref, norm_ref):
    wide = pick_ref.shape[0]
    keys, values = block_parts(kv_ref[...], pick_ref[...])
    scores = masked_scores(q_ref[0], keys, bias_ref[...], wide)
    is_high = high_ref[...] > 0.5
    high_max = jnp.max(jnp.where(is_high, scores, FAR), 1, keepdims=True)
    low_max = jnp.max(jnp.where(is_high, FAR, scores), 1, keepdims=True)
    terms = jnp.exp(scores - jnp.where(is_high, high_max, low_max))
    high_sum = jnp.sum(jnp.where(is_high, terms, 0.0), 1, keepdims=True)
    low_sum = jnp.sum(jnp.where(is_high, 0.0, terms), 1, keepdims=True)
    mixed = jnp.dot(terms.astype(jnp.bfloat16), values, preferred_element_type=jnp.float32)
    out_ref[0] = mixed / spread(high_sum, low_sum)
    norm_ref[0] = spread(high_max + jnp.log(high_sum), low_max + jnp.log(low_sum))


def backward_kernel(
    high_ref, pick_ref, bias_ref, q_ref, kv_ref, g_ref, out_ref, norm_ref, dq_ref, dkv_ref
):
    wide = pick_ref.shape[0]
    pick = pick_ref[...]
    queries, grads = q_ref[0], g_ref[0]
    keys, values = block_parts(kv_ref[...], pick)
    scores = masked_scores(queries, keys, bias_ref[...], wide)
    is_high = high_ref[...] > 0.5
    norm = norm_ref[0]
    probs = jnp.exp(scores - jnp.where(is_high, norm[:, :1], norm[:, HD : HD + 1]))
    product = grads.astype(jnp.float32) * out_ref[0]
    high_delta = jnp.sum(product[:, :HD], 1, keepdims=True)
    low_delta = jnp.sum(product[:, HD:], 1, keepdims=True)
    dprobs = lax.dot_general(
        grads, values, (((1,), (1,)), ((), ())), preferred_element_type=jnp.float32
    )
    dscores = (probs * (dprobs - jnp.where(is_high, high_delta, low_delta))).astype(jnp.bfloat16)
    dq_ref[0] = jnp.dot(dscores, keys, preferred_element_type=jnp.float32) * HD ** (-0.5)
    over_rows = (((0,), (0,)), ((), ()))
    dkeys = lax.dot_general(dscores, queries, over_rows, preferred_element_type=jnp.float32)
    dvalues = lax.dot_general(
        probs.astype(jnp.bfloat16), grads, over_rows, preferred_element_type=jnp.float32
    )
    pick_wide = pick.astype(jnp.float32)

    def fold(terms):
        low = terms[:wide, :HD] + terms[wide : 2 * wide, HD:] * (1.0 - pick_wide)
        own = low[:HD] + terms[2 * wide : 2 * wide + HD, HD:]
        return jnp.concatenate([own, low[HD:]], 0), terms[wide : 2 * wide, :HD] * pick_wide

    low_k, high_k = fold(dkeys)
    low_v, high_v = fold(dvalues)
    slots = wide // HD
    low = jnp.concatenate([low_k, low_v], 1).astype(jnp.bfloat16).reshape(slots, 1, HD, 2 * HD)
    high = jnp.concatenate([high_k, high_v], 1).astype(jnp.bfloat16).reshape(slots, 1, HD, 2 * HD)
    dkv_ref[...] = jnp.concatenate([low, high], 1).reshape(dkv_ref.shape)


def attention_call(kernel, consts, by_head, kv, backward):
    high_row, pick, bias = consts
    wide = pick.shape[0]
    rows = by_head[0].shape[1]
    whole = lambda array: pl.BlockSpec(array.shape, lambda g: (0, 0))
    head = pl.BlockSpec((1, rows, 2 * HD), lambda g: (g, 0, 0))
    kv_spec = pl.BlockSpec((kv.shape[0], 2 * HD), lambda g: (0, g))
    head_out = jax.ShapeDtypeStruct((KVH, rows, 2 * HD), jnp.float32)
    columns = 2 * wide + 2 * HD
    work = 2 * rows * columns * 2 * HD * KVH
    moved = KVH * rows * 2 * HD * 16 + kv.size * (4 if backward else 2)
    return pl.pallas_call(
        kernel,
        grid=(KVH,),
        in_specs=[whole(high_row), whole(pick), whole(bias), head, kv_spec]
        + [head] * (len(by_head) - 1),
        out_specs=[head, kv_spec if backward else head],
        out_shape=[head_out, jax.ShapeDtypeStruct(kv.shape, jnp.bfloat16) if backward else head_out],
        compiler_params=pltpu.CompilerParams(vmem_limit_bytes=52 * 1024 * 1024),
        cost_estimate=pl.CostEstimate(
            flops=work * (20 if backward else 8),
            bytes_accessed=moved,
            transcendentals=rows * columns * KVH,
        ),
    )(high_row, pick, bias, by_head[0], kv, *by_head[1:])


def stack_heads(flat):
    seqs = flat.shape[0]
    split = flat.reshape(seqs, 2, HD, KVH, GROUP, HD)[:, ::-1]
    return split.transpose(0, 3, 4, 2, 1, 5).reshape(seqs, KVH, GROUP * HD, 2 * HD)


def unstack_heads(stacked):
    seqs = stacked.shape[0]
    split = stacked.reshape(seqs, KVH, GROUP, HD, 2, HD).transpose(0, 4, 3, 1, 2, 5)[:, ::-1]
    return split.reshape(seqs, 2 * HD, QH * HD)


def body(
    layer_input,
    out_grad,
    attn_gain,
    w_query,
    w_key,
    w_value,
    w_output,
    mlp_gain,
    w_gate,
    w_up,
    w_down,
):
    size = lax.axis_size("ctx")
    c = lax.axis_index("ctx")
    core = c & 1
    q_width, kv_width = QH * HD, KVH * HD
    gains = jnp.stack([attn_gain, mlp_gain], 1)
    gains = jnp.pad(gains, ((0, 0), (0, HD - 2)))
    first_all = fsdp_gather(jnp.concatenate([w_query, w_key, w_value, gains], 1), core)
    output_all = fsdp_gather(w_output, core)
    gate_all = fsdp_gather(w_gate, core)
    up_all = fsdp_gather(w_up, core)
    down_all = fsdp_gather(w_down, core)
    proj_width = q_width + 2 * kv_width
    qkv_all = first_all[:, :proj_width]
    gain_first = first_all[:, proj_width].astype(jnp.float32)
    gain_mid = first_all[:, proj_width + 1].astype(jnp.float32)
    seq_count, shard_rows = (layer_input.shape[0], layer_input.shape[1])
    local_pos = place_rows(c * shard_rows, shard_rows, shard_rows, size)
    source = layer_input.astype(jnp.float32)
    inv_one = lax.rsqrt(jnp.mean(source * source, -1, keepdims=True) + EPS)
    normed_one = source * inv_one
    h_one = (normed_one * gain_first).astype(jnp.bfloat16)
    qkv = jnp.dot(h_one, qkv_all, preferred_element_type=jnp.float32)
    queries_flat = rotate(qkv[..., :q_width], local_pos, QH, 1.0).astype(jnp.bfloat16)
    keys_flat = rotate(qkv[..., q_width : q_width + kv_width], local_pos, KVH, 1.0)
    by_kv_head = (seq_count, shard_rows, KVH, HD)
    kv_local = jnp.concatenate(
        [
            keys_flat.astype(jnp.bfloat16).reshape(by_kv_head),
            qkv[..., q_width + kv_width :].astype(jnp.bfloat16).reshape(by_kv_head),
        ],
        -1,
    ).reshape(seq_count, shard_rows, 2 * kv_width)
    q_heads = stack_heads(queries_flat * jnp.bfloat16(HD ** (-0.5)))

    within = jnp.arange(GROUP * HD, dtype=jnp.int32)[:, None] % HD
    tile = jnp.arange(4 * HD, dtype=jnp.int32)[None, :]
    first_tile = (tile < HD) & (tile > within)
    spare_tile = (tile >= 2 * HD) & (tile - 2 * HD > within)
    bias = jnp.where(first_tile | spare_tile, FAR, 0.0).astype(jnp.float32)
    gathered, orders, consts = [], [], []
    for s in range(seq_count):
        masks = gather_order(size, s)
        pieces = kv_local[s]
        for mask in masks:
            pieces = jnp.concatenate([pieces, xor_permute(pieces, mask)], 0)
        picks = jnp.repeat((holders(size, masks) ^ c) >= c, HD)
        high_row = jnp.concatenate(
            [jnp.ones(size * HD, bool), picks, jnp.zeros(2 * HD, bool)]
        ).astype(jnp.float32)[None, :]
        pick = jnp.broadcast_to(picks[:, None], (size * HD, HD)).astype(jnp.bfloat16)
        gathered.append(pieces)
        orders.append(masks)
        consts.append((high_row, pick, bias))
    outs, norms = [], []
    for s in range(seq_count):
        out, norm = attention_call(forward_kernel, consts[s], (q_heads[s],), gathered[s], False)
        outs.append(out)
        norms.append(norm)
    attended = unstack_heads(jnp.stack(outs).astype(jnp.bfloat16))
    middle = source + jnp.dot(attended, output_all, preferred_element_type=jnp.float32)
    inv_two = lax.rsqrt(jnp.mean(middle * middle, -1, keepdims=True) + EPS)
    normed_two = middle * inv_two
    h_two = (normed_two * gain_mid).astype(jnp.bfloat16)
    gate = jnp.dot(h_two, gate_all, preferred_element_type=jnp.float32)
    up_proj = jnp.dot(h_two, up_all, preferred_element_type=jnp.float32)
    sigma = jax.nn.sigmoid(gate)
    silu_gate = gate * sigma
    hidden = (silu_gate * up_proj).astype(jnp.bfloat16)
    layer_output = (middle + jnp.dot(hidden, down_all, preferred_element_type=jnp.float32)).astype(
        jnp.bfloat16
    )
    g_hidden = times_transposed(out_grad, down_all)
    down_grad = outer_sum(hidden, out_grad)
    down_shard = reduce_grad(down_grad, 0)
    gate_slope = sigma * (1.0 + gate * (1.0 - sigma))
    g_gate = (g_hidden * up_proj * gate_slope).astype(jnp.bfloat16)
    g_up = (g_hidden * silu_gate).astype(jnp.bfloat16)
    gate_grad = outer_sum(h_two, g_gate)
    up_grad = outer_sum(h_two, g_up)
    gate_shard = reduce_grad(gate_grad, 1)
    up_shard = reduce_grad(up_grad, 1)
    g_h_two = times_transposed(g_gate, gate_all) + times_transposed(g_up, up_all)
    mlp_gain_grad = jnp.sum(g_h_two * normed_two, (0, 1))
    g_normed_two = g_h_two * gain_mid
    g_middle = out_grad.astype(jnp.float32) + inv_two * (
        g_normed_two - normed_two * jnp.mean(g_normed_two * normed_two, -1, keepdims=True)
    )
    g_branch = g_middle.astype(jnp.bfloat16)
    output_grad = outer_sum(attended, g_branch)
    output_shard = reduce_grad(output_grad, 0)
    g_attended = times_transposed(g_branch, output_all).astype(jnp.bfloat16)
    grad_heads = stack_heads(g_attended)
    dqueries, kv_grads = [], []
    for s in range(seq_count):
        dquery, term = attention_call(
            backward_kernel,
            consts[s],
            (q_heads[s], grad_heads[s], outs[s], norms[s]),
            gathered[s],
            True,
        )
        dqueries.append(dquery)
        for mask in orders[s][::-1]:
            half = term.shape[0] // 2
            term = add_low(term[:half], xor_permute(term[half:], mask))
        kv_grads.append(term)
    dquery_flat = unstack_heads(jnp.stack(dqueries))
    g_query_proj = rotate(dquery_flat, local_pos, QH, -1.0).astype(jnp.bfloat16)
    query_shard = reduce_grad(outer_sum(h_one, g_query_proj), 0)
    kv_grad = jnp.stack(kv_grads).reshape(seq_count, shard_rows, KVH, 2, HD)
    key_part = kv_grad[:, :, :, 0].reshape(seq_count, shard_rows, kv_width)
    g_key_proj = rotate(key_part.astype(jnp.float32), local_pos, KVH, -1.0).astype(jnp.bfloat16)
    g_value_proj = kv_grad[:, :, :, 1].reshape(seq_count, shard_rows, kv_width)
    g_kv = jnp.concatenate([g_key_proj, g_value_proj], -1)
    g_h_one = times_transposed(
        jnp.concatenate([g_query_proj, g_kv], -1), qkv_all
    )
    attn_gain_grad = jnp.sum(g_h_one * normed_one, (0, 1))
    gain_grads = jnp.pad(jnp.stack([attn_gain_grad, mlp_gain_grad], 1), ((0, 0), (0, HD - 2)))
    last_shard = reduce_grad(jnp.concatenate([outer_sum(h_one, g_kv), gain_grads], 1), 0)
    g_normed_one = g_h_one * gain_first
    input_grad = (
        g_middle
        + inv_one
        * (g_normed_one - normed_one * jnp.mean(g_normed_one * normed_one, -1, keepdims=True))
    ).astype(jnp.bfloat16)
    return (
        layer_output,
        input_grad,
        last_shard[:, 2 * kv_width],
        query_shard,
        last_shard[:, :kv_width],
        last_shard[:, kv_width : 2 * kv_width],
        output_shard,
        last_shard[:, 2 * kv_width + 1],
        gate_shard,
        up_shard,
        down_shard,
    )


def solution(mesh):
    in_specs = (
        P("fsdp", "ctx", None),
        P("fsdp", "ctx", None),
        P("fsdp"),
        P("fsdp", None),
        P("fsdp", None),
        P("fsdp", None),
        P("fsdp", None),
        P("fsdp"),
        P("fsdp", None),
        P("fsdp", None),
        P("fsdp", None),
    )
    out_specs = (
        P("fsdp", "ctx", None),
        P("fsdp", "ctx", None),
        P("fsdp"),
        P("fsdp", None),
        P("fsdp", None),
        P("fsdp", None),
        P("fsdp", None),
        P("fsdp"),
        P("fsdp", None),
        P("fsdp", None),
        P("fsdp", None),
    )
    return jax.shard_map(body, mesh=mesh, in_specs=in_specs, out_specs=out_specs, check_vma=False)
```

```python
import jax
import jax.numpy as jnp
from jax import lax
from jax.experimental import pallas as pl
from jax.experimental.pallas import tpu as pltpu
from jax.sharding import PartitionSpec as P

QH = 15
KVH = 5
HD = 64
GROUP = QH // KVH


EPS = 1e-05
THETA = 100000.0
FAR = -1e30


def place_rows(start_row, row_count, shard_rows, ctx_size):
    stored = start_row + jnp.arange(row_count, dtype=jnp.int32)
    half_rows = shard_rows // 2
    holder = stored // shard_rows
    within = stored % shard_rows
    mirror = (2 * ctx_size - 1 - holder) * half_rows + within - half_rows
    return jnp.where(within < half_rows, holder * half_rows + within, mirror)


def turn_tables(position, sign):
    frequency = THETA ** (-jnp.arange(0, HD, 2, dtype=jnp.float32) / HD)
    angles = position.astype(jnp.float32)[:, None] * frequency[None, :]
    cosine, sine = jnp.cos(angles), sign * jnp.sin(angles)
    cosine = jnp.concatenate([cosine, cosine], -1)
    sine = jnp.concatenate([-sine, sine], -1)
    still = jnp.ones_like(cosine)
    cosine = jnp.concatenate([cosine] * QH + [cosine, still] * KVH, -1)
    sine = jnp.concatenate([sine] * QH + [sine, 0.0 * still] * KVH, -1)
    return cosine, sine


def turn(flat, tables):
    cosine, sine = tables
    part = HD // 2
    after = jnp.concatenate([flat[..., part:], flat[..., :part]], -1)
    before = jnp.concatenate([flat[..., -part:], flat[..., :-part]], -1)
    first = jnp.arange(flat.shape[-1]) % HD < part
    return flat * cosine + jnp.where(first, after, before) * sine


def outer_sum(left, right):
    return lax.dot_general(
        left, right, (((0, 1), (0, 1)), ((), ())), preferred_element_type=jnp.float32
    )


def times_transposed(grad_in, weight):
    return lax.dot_general(
        grad_in, weight, (((2,), (1,)), ((), ())), preferred_element_type=jnp.float32
    )


def paired():
    size = lax.axis_size("ctx")
    return lax.axis_size("fsdp") == 2 and size >= 4 and not size & (size - 1)


def fetch_piece(shard):
    if not paired():
        return lax.all_gather(shard, "fsdp", axis=0, tiled=True)
    half = shard.shape[0] // 2
    core = lax.axis_index("ctx") & 1
    piece = lax.dynamic_slice_in_dim(shard, core * half, half, 0)
    return lax.ppermute(piece, "fsdp", [(0, 1), (1, 0)])


def fill_in(shard, got):
    if not paired():
        return got
    f = lax.axis_index("fsdp")
    core = lax.axis_index("ctx") & 1
    rows = shard.shape[0]
    half = rows // 2
    other = xor_permute(got, 1)
    full = jnp.zeros((2 * rows,) + shard.shape[1:], shard.dtype)
    full = lax.dynamic_update_slice_in_dim(full, shard, f * rows, 0)
    start = (1 - f) * rows
    full = lax.dynamic_update_slice_in_dim(full, got, start + core * half, 0)
    return lax.dynamic_update_slice_in_dim(full, other, start + (1 - core) * half, 0)


def xor_permute(array, mask):
    size = lax.axis_size("ctx")
    return lax.ppermute(array, "ctx", [(i, i ^ mask) for i in range(size)])


def add_low(kept, received):
    total = kept.astype(jnp.float32) + received.astype(jnp.float32)
    return total.astype(jnp.bfloat16)


def reduce_core(grad):
    grad = grad.astype(jnp.bfloat16)
    if not paired():
        return grad
    core = lax.axis_index("ctx") & 1
    rows, cols = grad.shape
    parts = grad.reshape(2, 2, rows // 4, cols)
    keep = lax.dynamic_index_in_dim(parts, core, 1, False)
    send = lax.dynamic_index_in_dim(parts, 1 - core, 1, False)
    return add_low(keep, xor_permute(send, 1))


def reduce_pair(total):
    if not paired():
        return lax.psum_scatter(total, "fsdp", scatter_dimension=0, tiled=True)
    f = lax.axis_index("fsdp")
    keep = lax.dynamic_index_in_dim(total, f, 0, False)
    send = lax.dynamic_index_in_dim(total, 1 - f, 0, False)
    return add_low(keep, lax.ppermute(send, "fsdp", [(0, 1), (1, 0)]))


def reduce_rest(total, split_dim):
    if not paired():
        return lax.psum(total, "ctx").astype(jnp.float32)
    size = lax.axis_size("ctx")
    c = lax.axis_index("ctx")
    masks = []
    mask = 2
    while mask < size:
        masks.append(mask)
        mask *= 2
    for mask in masks[:-1]:
        bit = (c // mask) % 2
        half = total.shape[split_dim] // 2
        keep = lax.dynamic_slice_in_dim(total, bit * half, half, split_dim)
        send = lax.dynamic_slice_in_dim(total, (1 - bit) * half, half, split_dim)
        total = add_low(keep, xor_permute(send, mask))
    total = add_low(total, xor_permute(total, masks[-1]))
    for mask in masks[:-1][::-1]:
        total = join(total, xor_permute(total, mask), (c // mask) % 2, split_dim)
    return join(total, xor_permute(total, 1), c & 1, 0).astype(jnp.float32)


def reduce_grad(grad, split_dim):
    return reduce_rest(reduce_pair(reduce_core(grad)), split_dim)


def after(arrays, *others):
    tied = lax.optimization_barrier((tuple(arrays), others))
    return tied[0]


def join(mine, theirs, bit, dim):
    first = jnp.where(bit == 0, mine, theirs)
    second = jnp.where(bit == 0, theirs, mine)
    return jnp.concatenate([first, second], dim)


def gather_order(size, which):
    masks = []
    mask = size // 2
    while mask:
        masks.append(mask)
        mask //= 2
    if which % 2 and len(masks) >= 4:
        masks[1:3] = masks[1:3][::-1]
    return masks


def holders(size, masks):
    offsets = [0]
    for mask in masks:
        offsets = offsets + [offset ^ mask for offset in offsets]
    return jnp.array(offsets, jnp.int32)


def block_parts(kv, pick):
    slots = kv.shape[0] // (4 * HD) * 2
    split = kv.reshape(slots, 2, HD, 2 * HD)
    low = split[:, 0].reshape(slots * HD, 2 * HD)
    high = split[:, 1].reshape(slots * HD, 2 * HD)
    nothing = jnp.zeros((slots * HD, HD), kv.dtype)
    nothing_own = jnp.zeros((2 * HD, HD), kv.dtype)
    rest = 1 - pick

    def of(at):
        lows, highs = low[:, at : at + HD], high[:, at : at + HD]
        return jnp.concatenate(
            [
                jnp.concatenate([nothing, lows], 1),
                jnp.concatenate([lows * rest, highs * pick], 1),
                jnp.concatenate([kv[: 2 * HD, at : at + HD], nothing_own], 1),
            ],
            0,
        )

    return of(0), of(HD)


def masked_scores(queries, keys, bias, wide):
    scores = lax.dot_general(
        queries, keys, (((1,), (1,)), ((), ())), preferred_element_type=jnp.float32
    )
    step = 2 * HD
    return jnp.concatenate(
        [
            scores[:, :wide],
            scores[:, wide : wide + step] + bias[:, :step],
            scores[:, wide + step : 2 * wide],
            scores[:, 2 * wide :] + bias[:, step:],
        ],
        1,
    )


def spread(low, high):
    shape = (high.shape[0], HD)
    return jnp.concatenate([jnp.broadcast_to(low, shape), jnp.broadcast_to(high, shape)], 1)


def stage_heads(flat_ref, staged_ref):
    for head in range(KVH):

        @pl.when(pl.program_id(0) == head)
        def _():
            for j in range(GROUP):
                at = (head * GROUP + j) * HD
                rows = slice(j * HD, (j + 1) * HD)
                staged_ref[rows, :HD] = flat_ref[0, :HD, at : at + HD]
                staged_ref[rows, HD:] = flat_ref[0, HD:, at : at + HD]


def unstage_heads(staged, flat_ref):
    for head in range(KVH):

        @pl.when(pl.program_id(0) == head)
        def _():
            for j in range(GROUP):
                at = (head * GROUP + j) * HD
                rows = slice(j * HD, (j + 1) * HD)
                flat_ref[:HD, at : at + HD] = staged[rows, :HD]
                flat_ref[HD:, at : at + HD] = staged[rows, HD:]


def forward_kernel(high_ref, pick_ref, bias_ref, q_ref, kv_ref, out_ref, norm_ref, flat_ref, q_rows):
    stage_heads(q_ref, q_rows)
    wide = pick_ref.shape[0]
    keys, values = block_parts(kv_ref[...], pick_ref[...])
    scores = masked_scores(q_rows[...], keys, bias_ref[...], wide)
    is_high = high_ref[...] > 0.5
    high_max = jnp.max(jnp.where(is_high, scores, FAR), 1, keepdims=True)
    low_max = jnp.max(jnp.where(is_high, FAR, scores), 1, keepdims=True)
    terms = jnp.exp(scores - jnp.where(is_high, high_max, low_max))
    high_sum = jnp.sum(jnp.where(is_high, terms, 0.0), 1, keepdims=True)
    low_sum = jnp.sum(jnp.where(is_high, 0.0, terms), 1, keepdims=True)
    mixed = jnp.dot(terms.astype(jnp.bfloat16), values, preferred_element_type=jnp.float32)
    mixed = mixed / spread(low_sum, high_sum)
    out_ref[0] = mixed
    unstage_heads(mixed.astype(jnp.bfloat16), flat_ref)
    norm_ref[0] = spread(low_max + jnp.log(low_sum), high_max + jnp.log(high_sum))


def backward_kernel(
    high_ref,
    pick_ref,
    bias_ref,
    q_ref,
    kv_ref,
    g_ref,
    out_ref,
    norm_ref,
    dq_ref,
    dkv_ref,
    q_rows,
    g_rows,
):
    stage_heads(q_ref, q_rows)
    stage_heads(g_ref, g_rows)
    wide = pick_ref.shape[0]
    pick = pick_ref[...]
    queries, grads = q_rows[...], g_rows[...]
    keys, values = block_parts(kv_ref[...], pick)
    scores = masked_scores(queries, keys, bias_ref[...], wide)
    is_high = high_ref[...] > 0.5
    norm = norm_ref[0]
    probs = jnp.exp(scores - jnp.where(is_high, norm[:, HD : HD + 1], norm[:, :1]))
    product = grads.astype(jnp.float32) * out_ref[0]
    high_delta = jnp.sum(product[:, HD:], 1, keepdims=True)
    low_delta = jnp.sum(product[:, :HD], 1, keepdims=True)
    dprobs = lax.dot_general(
        grads, values, (((1,), (1,)), ((), ())), preferred_element_type=jnp.float32
    )
    dscores = (probs * (dprobs - jnp.where(is_high, high_delta, low_delta))).astype(jnp.bfloat16)
    dquery = jnp.dot(dscores, keys, preferred_element_type=jnp.float32) * HD ** (-0.5)
    unstage_heads(dquery, dq_ref)
    over_rows = (((0,), (0,)), ((), ()))
    dkeys = lax.dot_general(dscores, queries, over_rows, preferred_element_type=jnp.float32)
    dvalues = lax.dot_general(
        probs.astype(jnp.bfloat16), grads, over_rows, preferred_element_type=jnp.float32
    )
    pick_wide = pick.astype(jnp.float32)

    def fold(terms):
        low = terms[:wide, HD:] + terms[wide : 2 * wide, :HD] * (1.0 - pick_wide)
        own = low[:HD] + terms[2 * wide : 2 * wide + HD, :HD]
        return jnp.concatenate([own, low[HD:]], 0), terms[wide : 2 * wide, HD:] * pick_wide

    low_k, high_k = fold(dkeys)
    low_v, high_v = fold(dvalues)
    slots = wide // HD
    low = jnp.concatenate([low_k, low_v], 1).astype(jnp.bfloat16).reshape(slots, 1, HD, 2 * HD)
    high = jnp.concatenate([high_k, high_v], 1).astype(jnp.bfloat16).reshape(slots, 1, HD, 2 * HD)
    dkv_ref[...] = jnp.concatenate([low, high], 1).reshape(dkv_ref.shape)


def attention_call(kernel, consts, flats, kept, kv, s, backward):
    high_row, pick, bias = consts
    wide = pick.shape[0]
    rows = GROUP * HD
    shard_rows, q_width = flats[0].shape[1:]
    whole = lambda array: pl.BlockSpec(array.shape, lambda g: (0, 0))
    flat = pl.BlockSpec((1, shard_rows, q_width), lambda g: (s, 0, 0))
    flat_out = pl.BlockSpec((shard_rows, q_width), lambda g: (0, 0))
    head = pl.BlockSpec((1, rows, 2 * HD), lambda g: (g, 0, 0))
    kv_spec = pl.BlockSpec((kv.shape[0], 2 * HD), lambda g: (0, g))
    head_shape = jax.ShapeDtypeStruct((KVH, rows, 2 * HD), jnp.float32)
    if backward:
        out_specs = [flat_out, kv_spec]
        out_shape = [
            jax.ShapeDtypeStruct((shard_rows, q_width), jnp.float32),
            jax.ShapeDtypeStruct(kv.shape, jnp.bfloat16),
        ]
    else:
        out_specs = [head, head, flat_out]
        out_shape = [
            head_shape,
            head_shape,
            jax.ShapeDtypeStruct((shard_rows, q_width), jnp.bfloat16),
        ]
    work = 2 * rows * (2 * wide + 2 * HD) * 2 * HD * KVH
    return pl.pallas_call(
        kernel,
        grid=(KVH,),
        in_specs=[whole(high_row), whole(pick), whole(bias), flat, kv_spec]
        + [flat] * (len(flats) - 1)
        + [head] * len(kept),
        out_specs=out_specs,
        out_shape=out_shape,
        scratch_shapes=[pltpu.VMEM((rows, 2 * HD), jnp.bfloat16)] * len(flats),
        compiler_params=pltpu.CompilerParams(vmem_limit_bytes=52 * 1024 * 1024),
        cost_estimate=pl.CostEstimate(
            flops=work * (80 if backward else 40),
            bytes_accessed=kv.size * (4 if backward else 2),
            transcendentals=rows * (2 * wide + 2 * HD) * KVH,
        ),
    )(high_row, pick, bias, flats[0], kv, *flats[1:], *kept)


def body(
    layer_input,
    out_grad,
    attn_gain,
    w_query,
    w_key,
    w_value,
    w_output,
    mlp_gain,
    w_gate,
    w_up,
    w_down,
):
    size = lax.axis_size("ctx")
    c = lax.axis_index("ctx")
    core = c & 1
    q_width, kv_width = QH * HD, KVH * HD
    gains = jnp.stack([attn_gain, mlp_gain], 1)
    gains = jnp.pad(gains, ((0, 0), (0, HD - 2)))
    pad_rows = w_key.shape[0]
    kv_weight = jnp.concatenate(
        [w_key.reshape(pad_rows, KVH, HD), w_value.reshape(pad_rows, KVH, HD)], -1
    ).reshape(pad_rows, 2 * kv_width)
    first = jnp.concatenate([w_query, kv_weight, gains], 1)
    first_got = fetch_piece(first)
    later = after((w_output, w_gate, w_up, w_down), first_got)
    later_got = [fetch_piece(weight) for weight in later]
    first_all = fill_in(first, first_got)
    proj_width = q_width + 2 * kv_width
    qkv_all = first_all[:, :proj_width]
    gain_first = first_all[:, proj_width].astype(jnp.float32)
    gain_mid = first_all[:, proj_width + 1].astype(jnp.float32)
    seq_count, shard_rows = (layer_input.shape[0], layer_input.shape[1])
    local_pos = place_rows(c * shard_rows, shard_rows, shard_rows, size)
    source = layer_input.astype(jnp.float32)
    inv_one = lax.rsqrt(jnp.mean(source * source, -1, keepdims=True) + EPS)
    normed_one = source * inv_one
    h_one = (normed_one * gain_first).astype(jnp.bfloat16)
    qkv = jnp.dot(h_one, qkv_all, preferred_element_type=jnp.float32)
    turned = turn(qkv, turn_tables(local_pos, 1.0)).astype(jnp.bfloat16)
    queries = turned[..., :q_width] * jnp.bfloat16(HD ** (-0.5))
    kv_local = turned[..., q_width:]

    within = jnp.arange(GROUP * HD, dtype=jnp.int32)[:, None] % HD
    tile = jnp.arange(4 * HD, dtype=jnp.int32)[None, :]
    first_tile = (tile < HD) & (tile > within)
    spare_tile = (tile >= 2 * HD) & (tile - 2 * HD > within)
    bias = jnp.where(first_tile | spare_tile, FAR, 0.0).astype(jnp.float32)
    gathered, orders, consts = [], [], []
    for s in range(seq_count):
        masks = gather_order(size, s)
        pieces = kv_local[s]
        for mask in masks:
            pieces = jnp.concatenate([pieces, xor_permute(pieces, mask)], 0)
        picks = jnp.repeat((holders(size, masks) ^ c) >= c, HD)
        high_row = jnp.concatenate(
            [jnp.ones(size * HD, bool), picks, jnp.zeros(2 * HD, bool)]
        ).astype(jnp.float32)[None, :]
        pick = jnp.broadcast_to(picks[:, None], (size * HD, HD)).astype(jnp.bfloat16)
        gathered.append(pieces)
        orders.append(masks)
        consts.append((high_row, pick, bias))
    kept, flats = [], []
    for s in range(seq_count):
        out, norm, flat = attention_call(
            forward_kernel, consts[s], (queries,), (), gathered[s], s, False
        )
        kept.append((out, norm))
        flats.append(flat)
    later_got = after(later_got, flats[min(1, seq_count - 1)])
    output_all, gate_all, up_all, down_all = [
        fill_in(shard, got) for shard, got in zip(later, later_got)
    ]
    attended = jnp.stack(flats)
    middle = source + jnp.dot(attended, output_all, preferred_element_type=jnp.float32)
    inv_two = lax.rsqrt(jnp.mean(middle * middle, -1, keepdims=True) + EPS)
    normed_two = middle * inv_two
    h_two = (normed_two * gain_mid).astype(jnp.bfloat16)
    gate = jnp.dot(h_two, gate_all, preferred_element_type=jnp.float32)
    up_proj = jnp.dot(h_two, up_all, preferred_element_type=jnp.float32)
    sigma = jax.nn.sigmoid(gate)
    silu_gate = gate * sigma
    hidden = (silu_gate * up_proj).astype(jnp.bfloat16)
    layer_output = (middle + jnp.dot(hidden, down_all, preferred_element_type=jnp.float32)).astype(
        jnp.bfloat16
    )
    g_hidden = times_transposed(out_grad, down_all)
    down_grad = outer_sum(hidden, out_grad)
    down_part = reduce_core(down_grad)
    gate_slope = sigma * (1.0 + gate * (1.0 - sigma))
    g_gate = (g_hidden * up_proj * gate_slope).astype(jnp.bfloat16)
    g_up = (g_hidden * silu_gate).astype(jnp.bfloat16)
    gate_grad = outer_sum(h_two, g_gate)
    up_grad = outer_sum(h_two, g_up)
    gate_part = reduce_core(gate_grad)
    up_part = reduce_core(up_grad)
    g_h_two = times_transposed(g_gate, gate_all) + times_transposed(g_up, up_all)
    mlp_gain_grad = jnp.sum(g_h_two * normed_two, (0, 1))
    g_normed_two = g_h_two * gain_mid
    g_middle = out_grad.astype(jnp.float32) + inv_two * (
        g_normed_two - normed_two * jnp.mean(g_normed_two * normed_two, -1, keepdims=True)
    )
    g_branch = g_middle.astype(jnp.bfloat16)
    output_grad = outer_sum(attended, g_branch)
    output_shard = reduce_grad(output_grad, 0)
    g_attended = times_transposed(g_branch, output_all).astype(jnp.bfloat16)
    (g_attended,) = after((g_attended,), down_part, gate_part, up_part)
    parts = [reduce_pair(part) for part in (down_part, gate_part, up_part)]
    dqueries, kv_grads = [], []
    for s in range(seq_count):
        grads = g_attended
        if s >= 2 and s - 2 < len(parts):
            (grads,) = after((grads,), parts[s - 2])
        dquery, term = attention_call(
            backward_kernel, consts[s], (queries, grads), kept[s], gathered[s], s, True
        )
        dqueries.append(dquery)
        for mask in orders[s][::-1]:
            half = term.shape[0] // 2
            term = add_low(term[:half], xor_permute(term[half:], mask))
        kv_grads.append(term)
    down_shard = reduce_rest(parts[0], 0)
    gate_shard = reduce_rest(parts[1], 1)
    up_shard = reduce_rest(parts[2], 1)
    cosine, sine = turn_tables(local_pos, -1.0)
    q_tables = (cosine[:, :q_width], sine[:, :q_width])
    kv_tables = (cosine[:, q_width:], sine[:, q_width:])
    g_query_proj = turn(jnp.stack(dqueries), q_tables).astype(jnp.bfloat16)
    query_shard = reduce_grad(outer_sum(h_one, g_query_proj), 0)
    g_kv = turn(jnp.stack(kv_grads).astype(jnp.float32), kv_tables).astype(jnp.bfloat16)
    g_h_one = times_transposed(
        jnp.concatenate([g_query_proj, g_kv], -1), qkv_all
    )
    attn_gain_grad = jnp.sum(g_h_one * normed_one, (0, 1))
    gain_grads = jnp.pad(jnp.stack([attn_gain_grad, mlp_gain_grad], 1), ((0, 0), (0, HD - 2)))
    last_shard = reduce_grad(jnp.concatenate([outer_sum(h_one, g_kv), gain_grads], 1), 0)
    kv_shard = last_shard[:, : 2 * kv_width].reshape(pad_rows, KVH, 2, HD)
    g_normed_one = g_h_one * gain_first
    input_grad = (
        g_middle
        + inv_one
        * (g_normed_one - normed_one * jnp.mean(g_normed_one * normed_one, -1, keepdims=True))
    ).astype(jnp.bfloat16)
    return (
        layer_output,
        input_grad,
        last_shard[:, 2 * kv_width],
        query_shard,
        kv_shard[:, :, 0].reshape(pad_rows, kv_width),
        kv_shard[:, :, 1].reshape(pad_rows, kv_width),
        output_shard,
        last_shard[:, 2 * kv_width + 1],
        gate_shard,
        up_shard,
        down_shard,
    )


def solution(mesh):
    in_specs = (
        P("fsdp", "ctx", None),
        P("fsdp", "ctx", None),
        P("fsdp"),
        P("fsdp", None),
        P("fsdp", None),
        P("fsdp", None),
        P("fsdp", None),
        P("fsdp"),
        P("fsdp", None),
        P("fsdp", None),
        P("fsdp", None),
    )
    out_specs = (
        P("fsdp", "ctx", None),
        P("fsdp", "ctx", None),
        P("fsdp"),
        P("fsdp", None),
        P("fsdp", None),
        P("fsdp", None),
        P("fsdp", None),
        P("fsdp"),
        P("fsdp", None),
        P("fsdp", None),
        P("fsdp", None),
    )
    return jax.shard_map(body, mesh=mesh, in_specs=in_specs, out_specs=out_specs, check_vma=False)
```

```python
import jax
import jax.numpy as jnp
from jax import lax
from jax.experimental import pallas as pl
from jax.experimental.pallas import tpu as pltpu
from jax.sharding import PartitionSpec as P

QH = 15
KVH = 5
HD = 64
GROUP = QH // KVH


EPS = 1e-05
THETA = 100000.0
FAR = -1e30


def place_rows(start_row, row_count, shard_rows, ctx_size):
    stored = start_row + jnp.arange(row_count, dtype=jnp.int32)
    half_rows = shard_rows // 2
    holder = stored // shard_rows
    within = stored % shard_rows
    mirror = (2 * ctx_size - 1 - holder) * half_rows + within - half_rows
    return jnp.where(within < half_rows, holder * half_rows + within, mirror)


def turn_tables(position, sign):
    frequency = THETA ** (-jnp.arange(0, HD, 2, dtype=jnp.float32) / HD)
    angles = position.astype(jnp.float32)[:, None] * frequency[None, :]
    cosine, sine = jnp.cos(angles), sign * jnp.sin(angles)
    cosine = jnp.concatenate([cosine, cosine], -1)
    sine = jnp.concatenate([-sine, sine], -1)
    still = jnp.ones_like(cosine)
    cosine = jnp.concatenate([cosine] * QH + [cosine, still] * KVH, -1)
    sine = jnp.concatenate([sine] * QH + [sine, 0.0 * still] * KVH, -1)
    return cosine, sine


def turn(flat, tables):
    cosine, sine = tables
    part = HD // 2
    after = jnp.concatenate([flat[..., part:], flat[..., :part]], -1)
    before = jnp.concatenate([flat[..., -part:], flat[..., :-part]], -1)
    first = jnp.arange(flat.shape[-1]) % HD < part
    return flat * cosine + jnp.where(first, after, before) * sine


def outer_sum(left, right):
    return lax.dot_general(
        left, right, (((0, 1), (0, 1)), ((), ())), preferred_element_type=jnp.float32
    )


def times_transposed(grad_in, weight):
    return lax.dot_general(
        grad_in, weight, (((2,), (1,)), ((), ())), preferred_element_type=jnp.float32
    )


def paired():
    size = lax.axis_size("ctx")
    return lax.axis_size("fsdp") == 2 and size >= 4 and not size & (size - 1)


def fetch_piece(shard):
    if not paired():
        return lax.all_gather(shard, "fsdp", axis=0, tiled=True)
    half = shard.shape[0] // 2
    core = lax.axis_index("ctx") & 1
    piece = lax.dynamic_slice_in_dim(shard, core * half, half, 0)
    return lax.ppermute(piece, "fsdp", [(0, 1), (1, 0)])


def fill_in(shard, got):
    if not paired():
        return got
    f = lax.axis_index("fsdp")
    core = lax.axis_index("ctx") & 1
    rows = shard.shape[0]
    half = rows // 2
    other = xor_permute(got, 1)
    full = jnp.zeros((2 * rows,) + shard.shape[1:], shard.dtype)
    full = lax.dynamic_update_slice_in_dim(full, shard, f * rows, 0)
    start = (1 - f) * rows
    full = lax.dynamic_update_slice_in_dim(full, got, start + core * half, 0)
    return lax.dynamic_update_slice_in_dim(full, other, start + (1 - core) * half, 0)


def xor_permute(array, mask):
    size = lax.axis_size("ctx")
    return lax.ppermute(array, "ctx", [(i, i ^ mask) for i in range(size)])


def add_low(kept, received):
    total = kept.astype(jnp.float32) + received.astype(jnp.float32)
    return total.astype(jnp.bfloat16)


def reduce_core(grad):
    grad = grad.astype(jnp.bfloat16)
    if not paired():
        return grad
    core = lax.axis_index("ctx") & 1
    rows, cols = grad.shape
    parts = grad.reshape(2, 2, rows // 4, cols)
    keep = lax.dynamic_index_in_dim(parts, core, 1, False)
    send = lax.dynamic_index_in_dim(parts, 1 - core, 1, False)
    return add_low(keep, xor_permute(send, 1))


def reduce_pair(total):
    if not paired():
        return lax.psum_scatter(total, "fsdp", scatter_dimension=0, tiled=True)
    f = lax.axis_index("fsdp")
    keep = lax.dynamic_index_in_dim(total, f, 0, False)
    send = lax.dynamic_index_in_dim(total, 1 - f, 0, False)
    return add_low(keep, lax.ppermute(send, "fsdp", [(0, 1), (1, 0)]))


def reduce_rest(total, split_dim, swapped=False):
    if not paired():
        return lax.psum(total, "ctx").astype(jnp.float32)
    size = lax.axis_size("ctx")
    c = lax.axis_index("ctx")
    masks = []
    mask = 2
    while mask < size:
        masks.append(mask)
        mask *= 2
    if swapped and len(masks) > 2:
        masks[:2] = masks[:2][::-1]
    for mask in masks[:-1]:
        bit = (c // mask) % 2
        half = total.shape[split_dim] // 2
        keep = lax.dynamic_slice_in_dim(total, bit * half, half, split_dim)
        send = lax.dynamic_slice_in_dim(total, (1 - bit) * half, half, split_dim)
        total = add_low(keep, xor_permute(send, mask))
    total = add_low(total, xor_permute(total, masks[-1]))
    for mask in masks[:-1][::-1]:
        total = join(total, xor_permute(total, mask), (c // mask) % 2, split_dim)
    return join(total, xor_permute(total, 1), c & 1, 0).astype(jnp.float32)


def reduce_grad(grad, split_dim):
    return reduce_rest(reduce_pair(reduce_core(grad)), split_dim)


def after(arrays, *others):
    tied = lax.optimization_barrier((tuple(arrays), others))
    return tied[0]


def join(mine, theirs, bit, dim):
    first = jnp.where(bit == 0, mine, theirs)
    second = jnp.where(bit == 0, theirs, mine)
    return jnp.concatenate([first, second], dim)


def gather_order(size, which):
    masks = []
    mask = size // 2
    while mask:
        masks.append(mask)
        mask //= 2
    if which % 2 and len(masks) >= 4:
        masks[1:3] = masks[1:3][::-1]
    return masks


def holders(size, masks):
    offsets = [0]
    for mask in masks:
        offsets = offsets + [offset ^ mask for offset in offsets]
    return jnp.array(offsets, jnp.int32)


def block_parts(kv, pick):
    slots = kv.shape[0] // (4 * HD) * 2
    split = kv.reshape(slots, 2, HD, 2 * HD)
    low = split[:, 0].reshape(slots * HD, 2 * HD)
    high = split[:, 1].reshape(slots * HD, 2 * HD)
    nothing = jnp.zeros((slots * HD, HD), kv.dtype)
    nothing_own = jnp.zeros((2 * HD, HD), kv.dtype)
    rest = 1 - pick

    def of(at):
        lows, highs = low[:, at : at + HD], high[:, at : at + HD]
        return jnp.concatenate(
            [
                jnp.concatenate([nothing, lows], 1),
                jnp.concatenate([lows * rest, highs * pick], 1),
                jnp.concatenate([kv[: 2 * HD, at : at + HD], nothing_own], 1),
            ],
            0,
        )

    return of(0), of(HD)


def masked_scores(queries, keys, bias, wide):
    scores = lax.dot_general(
        queries, keys, (((1,), (1,)), ((), ())), preferred_element_type=jnp.float32
    )
    step = 2 * HD
    return jnp.concatenate(
        [
            scores[:, :wide],
            scores[:, wide : wide + step] + bias[:, :step],
            scores[:, wide + step : 2 * wide],
            scores[:, 2 * wide :] + bias[:, step:],
        ],
        1,
    )


def spread(low, high):
    shape = (high.shape[0], HD)
    return jnp.concatenate([jnp.broadcast_to(low, shape), jnp.broadcast_to(high, shape)], 1)


def stage_heads(flat_ref, staged_ref):
    for head in range(KVH):

        @pl.when(pl.program_id(0) == head)
        def _():
            for j in range(GROUP):
                at = (head * GROUP + j) * HD
                rows = slice(j * HD, (j + 1) * HD)
                staged_ref[rows, :HD] = flat_ref[0, :HD, at : at + HD]
                staged_ref[rows, HD:] = flat_ref[0, HD:, at : at + HD]


def unstage_heads(staged, flat_ref):
    for head in range(KVH):

        @pl.when(pl.program_id(0) == head)
        def _():
            for j in range(GROUP):
                at = (head * GROUP + j) * HD
                rows = slice(j * HD, (j + 1) * HD)
                flat_ref[:HD, at : at + HD] = staged[rows, :HD]
                flat_ref[HD:, at : at + HD] = staged[rows, HD:]


def forward_kernel(high_ref, pick_ref, bias_ref, q_ref, kv_ref, out_ref, norm_ref, flat_ref, q_rows):
    stage_heads(q_ref, q_rows)
    wide = pick_ref.shape[0]
    keys, values = block_parts(kv_ref[...], pick_ref[...])
    scores = masked_scores(q_rows[...], keys, bias_ref[...], wide)
    is_high = high_ref[...] > 0.5
    high_max = jnp.max(jnp.where(is_high, scores, FAR), 1, keepdims=True)
    low_max = jnp.max(jnp.where(is_high, FAR, scores), 1, keepdims=True)
    terms = jnp.exp(scores - jnp.where(is_high, high_max, low_max))
    high_sum = jnp.sum(jnp.where(is_high, terms, 0.0), 1, keepdims=True)
    low_sum = jnp.sum(jnp.where(is_high, 0.0, terms), 1, keepdims=True)
    mixed = jnp.dot(terms.astype(jnp.bfloat16), values, preferred_element_type=jnp.float32)
    mixed = mixed / spread(low_sum, high_sum)
    out_ref[0] = mixed
    unstage_heads(mixed.astype(jnp.bfloat16), flat_ref)
    norm_ref[0] = spread(low_max + jnp.log(low_sum), high_max + jnp.log(high_sum))


def backward_kernel(
    high_ref,
    pick_ref,
    bias_ref,
    q_ref,
    kv_ref,
    g_ref,
    out_ref,
    norm_ref,
    dq_ref,
    dkv_ref,
    q_rows,
    g_rows,
):
    stage_heads(q_ref, q_rows)
    stage_heads(g_ref, g_rows)
    wide = pick_ref.shape[0]
    pick = pick_ref[...]
    queries, grads = q_rows[...], g_rows[...]
    keys, values = block_parts(kv_ref[...], pick)
    scores = masked_scores(queries, keys, bias_ref[...], wide)
    is_high = high_ref[...] > 0.5
    norm = norm_ref[0]
    probs = jnp.exp(scores - jnp.where(is_high, norm[:, HD : HD + 1], norm[:, :1]))
    product = grads.astype(jnp.float32) * out_ref[0]
    high_delta = jnp.sum(product[:, HD:], 1, keepdims=True)
    low_delta = jnp.sum(product[:, :HD], 1, keepdims=True)
    dprobs = lax.dot_general(
        grads, values, (((1,), (1,)), ((), ())), preferred_element_type=jnp.float32
    )
    dscores = (probs * (dprobs - jnp.where(is_high, high_delta, low_delta))).astype(jnp.bfloat16)
    dquery = jnp.dot(dscores, keys, preferred_element_type=jnp.float32) * HD ** (-0.5)
    unstage_heads(dquery, dq_ref)
    over_rows = (((0,), (0,)), ((), ()))
    dkeys = lax.dot_general(dscores, queries, over_rows, preferred_element_type=jnp.float32)
    dvalues = lax.dot_general(
        probs.astype(jnp.bfloat16), grads, over_rows, preferred_element_type=jnp.float32
    )
    pick_wide = pick.astype(jnp.float32)

    def fold(terms):
        low = terms[:wide, HD:] + terms[wide : 2 * wide, :HD] * (1.0 - pick_wide)
        own = low[:HD] + terms[2 * wide : 2 * wide + HD, :HD]
        return jnp.concatenate([own, low[HD:]], 0), terms[wide : 2 * wide, HD:] * pick_wide

    low_k, high_k = fold(dkeys)
    low_v, high_v = fold(dvalues)
    slots = wide // HD
    low = jnp.concatenate([low_k, low_v], 1).astype(jnp.bfloat16).reshape(slots, 1, HD, 2 * HD)
    high = jnp.concatenate([high_k, high_v], 1).astype(jnp.bfloat16).reshape(slots, 1, HD, 2 * HD)
    dkv_ref[...] = jnp.concatenate([low, high], 1).reshape(dkv_ref.shape)


def attention_call(kernel, consts, flats, kept, kv, s, backward):
    high_row, pick, bias = consts
    wide = pick.shape[0]
    rows = GROUP * HD
    shard_rows, q_width = flats[0].shape[1:]
    whole = lambda array: pl.BlockSpec(array.shape, lambda g: (0, 0))
    flat = pl.BlockSpec((1, shard_rows, q_width), lambda g: (s, 0, 0))
    flat_out = pl.BlockSpec((shard_rows, q_width), lambda g: (0, 0))
    head = pl.BlockSpec((1, rows, 2 * HD), lambda g: (g, 0, 0))
    kv_spec = pl.BlockSpec((kv.shape[0], 2 * HD), lambda g: (0, g))
    head_shape = jax.ShapeDtypeStruct((KVH, rows, 2 * HD), jnp.float32)
    if backward:
        out_specs = [flat_out, kv_spec]
        out_shape = [
            jax.ShapeDtypeStruct((shard_rows, q_width), jnp.float32),
            jax.ShapeDtypeStruct(kv.shape, jnp.bfloat16),
        ]
    else:
        out_specs = [head, head, flat_out]
        out_shape = [
            head_shape,
            head_shape,
            jax.ShapeDtypeStruct((shard_rows, q_width), jnp.bfloat16),
        ]
    work = 2 * rows * (2 * wide + 2 * HD) * 2 * HD * KVH
    return pl.pallas_call(
        kernel,
        grid=(KVH,),
        in_specs=[whole(high_row), whole(pick), whole(bias), flat, kv_spec]
        + [flat] * (len(flats) - 1)
        + [head] * len(kept),
        out_specs=out_specs,
        out_shape=out_shape,
        scratch_shapes=[pltpu.VMEM((rows, 2 * HD), jnp.bfloat16)] * len(flats),
        compiler_params=pltpu.CompilerParams(vmem_limit_bytes=52 * 1024 * 1024),
        cost_estimate=pl.CostEstimate(
            flops=work * (80 if backward else 40),
            bytes_accessed=kv.size * (4 if backward else 2),
            transcendentals=rows * (2 * wide + 2 * HD) * KVH,
        ),
    )(high_row, pick, bias, flats[0], kv, *flats[1:], *kept)


def body(
    layer_input,
    out_grad,
    attn_gain,
    w_query,
    w_key,
    w_value,
    w_output,
    mlp_gain,
    w_gate,
    w_up,
    w_down,
):
    size = lax.axis_size("ctx")
    c = lax.axis_index("ctx")
    core = c & 1
    q_width, kv_width = QH * HD, KVH * HD
    gains = jnp.stack([attn_gain, mlp_gain], 1)
    gains = jnp.pad(gains, ((0, 0), (0, HD - 2)))
    pad_rows = w_key.shape[0]
    kv_weight = jnp.concatenate(
        [w_key.reshape(pad_rows, KVH, HD), w_value.reshape(pad_rows, KVH, HD)], -1
    ).reshape(pad_rows, 2 * kv_width)
    first = jnp.concatenate([w_query, kv_weight, gains], 1)
    first_got = fetch_piece(first)
    later = after((w_output, w_gate, w_up, w_down), first_got)
    later_got = [fetch_piece(weight) for weight in later]
    first_all = fill_in(first, first_got)
    proj_width = q_width + 2 * kv_width
    qkv_all = first_all[:, :proj_width]
    gain_first = first_all[:, proj_width].astype(jnp.float32)
    gain_mid = first_all[:, proj_width + 1].astype(jnp.float32)
    seq_count, shard_rows = (layer_input.shape[0], layer_input.shape[1])
    local_pos = place_rows(c * shard_rows, shard_rows, shard_rows, size)
    source = layer_input.astype(jnp.float32)
    inv_one = lax.rsqrt(jnp.mean(source * source, -1, keepdims=True) + EPS)
    normed_one = source * inv_one
    h_one = (normed_one * gain_first).astype(jnp.bfloat16)
    qkv = jnp.dot(h_one, qkv_all, preferred_element_type=jnp.float32)
    turned = turn(qkv, turn_tables(local_pos, 1.0)).astype(jnp.bfloat16)
    queries = turned[..., :q_width] * jnp.bfloat16(HD ** (-0.5))
    kv_local = turned[..., q_width:]

    within = jnp.arange(GROUP * HD, dtype=jnp.int32)[:, None] % HD
    tile = jnp.arange(4 * HD, dtype=jnp.int32)[None, :]
    first_tile = (tile < HD) & (tile > within)
    spare_tile = (tile >= 2 * HD) & (tile - 2 * HD > within)
    bias = jnp.where(first_tile | spare_tile, FAR, 0.0).astype(jnp.float32)
    gathered, orders, consts = [], [], []
    for s in range(seq_count):
        masks = gather_order(size, s)
        pieces = kv_local[s]
        for step, mask in enumerate(masks):
            if step == 2 and s < 3:
                (pieces,) = after((pieces,), later_got[(0, 3, 1)[s]])
            pieces = jnp.concatenate([pieces, xor_permute(pieces, mask)], 0)
        picks = jnp.repeat((holders(size, masks) ^ c) >= c, HD)
        high_row = jnp.concatenate(
            [jnp.ones(size * HD, bool), picks, jnp.zeros(2 * HD, bool)]
        ).astype(jnp.float32)[None, :]
        pick = jnp.broadcast_to(picks[:, None], (size * HD, HD)).astype(jnp.bfloat16)
        gathered.append(pieces)
        orders.append(masks)
        consts.append((high_row, pick, bias))
    kept, flats = [], []
    for s in range(seq_count):
        fed = queries if s != 1 else after((queries,), later_got[2])[0]
        out, norm, flat = attention_call(
            forward_kernel, consts[s], (fed,), (), gathered[s], s, False
        )
        kept.append((out, norm))
        flats.append(flat)
    later_got = after(later_got, flats[min(1, seq_count - 1)])
    output_all, gate_all, up_all, down_all = [
        fill_in(shard, got) for shard, got in zip(later, later_got)
    ]
    attended = jnp.stack(flats)
    middle = source + jnp.dot(attended, output_all, preferred_element_type=jnp.float32)
    inv_two = lax.rsqrt(jnp.mean(middle * middle, -1, keepdims=True) + EPS)
    normed_two = middle * inv_two
    h_two = (normed_two * gain_mid).astype(jnp.bfloat16)
    gate = jnp.dot(h_two, gate_all, preferred_element_type=jnp.float32)
    up_proj = jnp.dot(h_two, up_all, preferred_element_type=jnp.float32)
    sigma = jax.nn.sigmoid(gate)
    silu_gate = gate * sigma
    hidden = (silu_gate * up_proj).astype(jnp.bfloat16)
    layer_output = (middle + jnp.dot(hidden, down_all, preferred_element_type=jnp.float32)).astype(
        jnp.bfloat16
    )
    g_hidden = times_transposed(out_grad, down_all)
    down_grad = outer_sum(hidden, out_grad)
    down_part = reduce_core(down_grad)
    gate_slope = sigma * (1.0 + gate * (1.0 - sigma))
    g_gate = (g_hidden * up_proj * gate_slope).astype(jnp.bfloat16)
    g_up = (g_hidden * silu_gate).astype(jnp.bfloat16)
    gate_grad = outer_sum(h_two, g_gate)
    up_grad = outer_sum(h_two, g_up)
    gate_part = reduce_core(gate_grad)
    up_part = reduce_core(up_grad)
    g_h_two = times_transposed(g_gate, gate_all) + times_transposed(g_up, up_all)
    mlp_gain_grad = jnp.sum(g_h_two * normed_two, (0, 1))
    g_normed_two = g_h_two * gain_mid
    g_middle = out_grad.astype(jnp.float32) + inv_two * (
        g_normed_two - normed_two * jnp.mean(g_normed_two * normed_two, -1, keepdims=True)
    )
    g_branch = g_middle.astype(jnp.bfloat16)
    output_grad = outer_sum(attended, g_branch)
    output_shard = reduce_grad(output_grad, 0)
    g_attended = times_transposed(g_branch, output_all).astype(jnp.bfloat16)
    (g_attended,) = after((g_attended,), down_part, gate_part, up_part)
    parts = [reduce_pair(part) for part in (down_part, gate_part, up_part)]
    dqueries, kv_grads = [], []
    for s in range(seq_count):
        grads = g_attended
        if s >= 2 and s - 2 < len(parts):
            (grads,) = after((grads,), parts[s - 2])
        dquery, term = attention_call(
            backward_kernel, consts[s], (queries, grads), kept[s], gathered[s], s, True
        )
        dqueries.append(dquery)
        for mask in orders[s][::-1]:
            half = term.shape[0] // 2
            term = add_low(term[:half], xor_permute(term[half:], mask))
        kv_grads.append(term)
    parts = after(parts, *kv_grads[-2:])
    down_shard = reduce_rest(parts[0], 0)
    gate_shard = reduce_rest(parts[1], 1, True)
    up_shard = reduce_rest(parts[2], 1)
    cosine, sine = turn_tables(local_pos, -1.0)
    q_tables = (cosine[:, :q_width], sine[:, :q_width])
    kv_tables = (cosine[:, q_width:], sine[:, q_width:])
    g_query_proj = turn(jnp.stack(dqueries), q_tables).astype(jnp.bfloat16)
    query_shard = reduce_grad(outer_sum(h_one, g_query_proj), 0)
    g_kv = turn(jnp.stack(kv_grads).astype(jnp.float32), kv_tables).astype(jnp.bfloat16)
    g_h_one = times_transposed(
        jnp.concatenate([g_query_proj, g_kv], -1), qkv_all
    )
    attn_gain_grad = jnp.sum(g_h_one * normed_one, (0, 1))
    gain_grads = jnp.pad(jnp.stack([attn_gain_grad, mlp_gain_grad], 1), ((0, 0), (0, HD - 2)))
    last_shard = reduce_grad(jnp.concatenate([outer_sum(h_one, g_kv), gain_grads], 1), 0)
    kv_shard = last_shard[:, : 2 * kv_width].reshape(pad_rows, KVH, 2, HD)
    g_normed_one = g_h_one * gain_first
    input_grad = (
        g_middle
        + inv_one
        * (g_normed_one - normed_one * jnp.mean(g_normed_one * normed_one, -1, keepdims=True))
    ).astype(jnp.bfloat16)
    return (
        layer_output,
        input_grad,
        last_shard[:, 2 * kv_width],
        query_shard,
        kv_shard[:, :, 0].reshape(pad_rows, kv_width),
        kv_shard[:, :, 1].reshape(pad_rows, kv_width),
        output_shard,
        last_shard[:, 2 * kv_width + 1],
        gate_shard,
        up_shard,
        down_shard,
    )


def solution(mesh):
    in_specs = (
        P("fsdp", "ctx", None),
        P("fsdp", "ctx", None),
        P("fsdp"),
        P("fsdp", None),
        P("fsdp", None),
        P("fsdp", None),
        P("fsdp", None),
        P("fsdp"),
        P("fsdp", None),
        P("fsdp", None),
        P("fsdp", None),
    )
    out_specs = (
        P("fsdp", "ctx", None),
        P("fsdp", "ctx", None),
        P("fsdp"),
        P("fsdp", None),
        P("fsdp", None),
        P("fsdp", None),
        P("fsdp", None),
        P("fsdp"),
        P("fsdp", None),
        P("fsdp", None),
        P("fsdp", None),
    )
    return jax.shard_map(body, mesh=mesh, in_specs=in_specs, out_specs=out_specs, check_vma=False)
```
